32 devices in a mesh: dp: 8 (over y, x, core), mp: 4 (over z).
Axes of the slice: x: 2, y: 2, z: 4, core: 2. Of those that a mesh axis runs over, the one named last changes fastest.
Arguments:
- inputs: bfloat16 [32768, 1024], P('dp'), may hold values from -6 to 6
- text_states: bfloat16 [32, 128, 1024], P('dp'), may hold values from -6 to 6
- text_lengths: int32 [32], P('dp'), may hold values from 8 to 128, as said below
- norm1_gain: float32 [1024], replicated, may hold values from 0.1 to 1.9
- norm1_bias: float32 [1024], replicated, may hold values from -2.5 to 2.5
- self_query: bfloat16 [1024, 1024], P(None, 'mp'), may hold values from -0.1875 to 0.1875
- self_key: bfloat16 [1024, 1024], P(None, 'mp'), may hold values from -0.1875 to 0.1875
- self_value: bfloat16 [1024, 1024], P(None, 'mp'), may hold values from -0.1875 to 0.1875
- self_out: bfloat16 [1024, 1024], P('mp'), may hold values from -3 to 3
- self_out_bias: float32 [1024], replicated, may hold values from -2.5 to 2.5
- norm2_gain: float32 [1024], replicated, may hold values from 0.1 to 1.9
- norm2_bias: float32 [1024], replicated, may hold values from -2.5 to 2.5
- cross_query: bfloat16 [1024, 1024], P(None, 'mp'), may hold values from -0.1875 to 0.1875
- cross_key: bfloat16 [1024, 1024], P(None, 'mp'), may hold values from -0.1875 to 0.1875
- cross_value: bfloat16 [1024, 1024], P(None, 'mp'), may hold values from -0.1875 to 0.1875
- cross_out: bfloat16 [1024, 1024], P('mp'), may hold values from -1 to 1
- cross_out_bias: float32 [1024], replicated, may hold values from -2.5 to 2.5
- norm3_gain: float32 [1024], replicated, may hold values from 0.1 to 1.9
- norm3_bias: float32 [1024], replicated, may hold values from -2.5 to 2.5
- mlp_in: bfloat16 [1024, 4096], P(None, 'mp'), may hold values from -0.1875 to 0.1875
- mlp_in_bias: float32 [4096], P('mp'), may hold values from -4 to 4
- mlp_out: bfloat16 [4096, 1024], P('mp'), may hold values from -0.125 to 0.125
- mlp_out_bias: float32 [1024], replicated, may hold values from -2.5 to 2.5
- cotangent: bfloat16 [32768, 1024], P('dp'), may hold values from -6 to 6
Outputs:
- output: bfloat16 [32768, 1024], P('dp')
- input_grad: bfloat16 [32768, 1024], P('dp')
- text_grad: float32 [32, 128, 1024], P('dp')
- norm1_gain_grad: float32 [1024], replicated
- norm1_bias_grad: float32 [1024], replicated
- self_query_grad: float32 [1024, 1024], P(None, 'mp')
- self_key_grad: float32 [1024, 1024], P(None, 'mp')
- self_value_grad: float32 [1024, 1024], P(None, 'mp')
- self_out_grad: float32 [1024, 1024], P('mp')
- self_out_bias_grad: float32 [1024], replicated
- norm2_gain_grad: float32 [1024], replicated
- norm2_bias_grad: float32 [1024], replicated
- cross_query_grad: float32 [1024, 1024], P(None, 'mp')
- cross_key_grad: float32 [1024, 1024], P(None, 'mp')
- cross_value_grad: float32 [1024, 1024], P(None, 'mp')
- cross_out_grad: float32 [1024, 1024], P('mp')
- cross_out_bias_grad: float32 [1024], replicated
- norm3_gain_grad: float32 [1024], replicated
- norm3_bias_grad: float32 [1024], replicated
- mlp_in_grad: float32 [1024, 4096], P(None, 'mp')
- mlp_in_bias_grad: float32 [4096], P('mp')
- mlp_out_grad: float32 [4096, 1024], P('mp')
- mlp_out_bias_grad: float32 [1024], replicated
The draws below stay inside these ranges and needn't reach their ends.
Inputs may be any that keep to these rules, and one draw needn't show every extreme that they name: `text_lengths`: valid text slots of each item; the slots after them are padding. Some item has all 128.
All inputs are finite; a program needn't handle non-finite values.
Results may differ from the reference program's by a relative error of at most 0.02.
The reference program's roundings to bfloat16 on the way count: a program that leaves them out, or rounds other values in their place, can miss the bound.
Values may be sent and summed in bfloat16 or wider, within the bound.
No kernel may reach another device: no remote copies, remote signals or barrier semaphores. Data moves between devices by JAX's collectives and lax.ppermute only.
A program may use at most 448 MiB of HBM per device.

```python
import jax
import jax.numpy as jnp
from jax import lax

D = 1024
HEADS = 16
HEAD_DIM = 64
FF = 4096
TXT = 128
SEQ = 1024
ITEMS = 32
TOKENS = 32768


def draw_text_lengths(key, part):
    key = jax.random.fold_in(key, 11)
    keys_split = jax.random.split(key, 4)
    lower_bound = max(TXT // 16, 1)
    longish = jax.random.randint(keys_split[0], (ITEMS,), TXT // 2 + 1, TXT + 1)
    shortish = jax.random.randint(keys_split[1], (ITEMS,), lower_bound, TXT // 2 + 1)
    selector = jax.random.randint(keys_split[2], (ITEMS,), 0, 4)
    lengths = jnp.where(selector == 0, shortish, longish)
    chosen = jax.random.randint(keys_split[3], (), 0, ITEMS)
    return jnp.where(jnp.arange(ITEMS) == chosen, TXT, lengths).astype(jnp.int32)


def steps_of(rng, extent, shards, smallest, high):
    factor_of, own = 1.0, jax.random.fold_in(rng, 6)
    for axis_at, parts in shards:
        heights = jnp.exp(jax.random.uniform(jax.random.fold_in(own, axis_at), (parts,), jnp.float32, smallest / len(shards), high / len(shards)))
        factor_of = factor_of * jnp.repeat(heights, extent[axis_at] // parts).reshape([-1 if axis == axis_at else 1 for axis in range(len(extent))])
    return factor_of


def noise(own_key, extent, width, reach, cuts=(), held_as=jnp.bfloat16):
    values = width * jax.random.normal(own_key, extent, jnp.float32)
    if cuts:
        values = values * steps_of(own_key, extent, cuts, -0.22, 0.18)
    return jnp.clip(values, -reach, reach).astype(held_as)


def setup_inputs(seed: int = 0) -> dict:
    key_list = jax.random.split(jax.random.key(seed), 25)
    return {
        "inputs": noise(key_list[0], (TOKENS, D), 1.0, 6.0, ((0, 8),)),
        "text_states": noise(key_list[1], (ITEMS, TXT, D), 1.0, 6.0, ((0, 8),)),
        "text_lengths": draw_text_lengths(jax.random.fold_in(key_list[24], 71), 0),
        "norm1_gain": jnp.clip(1.0 + 0.18 * jax.random.normal(key_list[3], (D,), jnp.float32), 0.1, 1.9),
        "norm1_bias": noise(key_list[4], (D,), 0.5, 2.5, (), jnp.float32),
        "self_query": noise(key_list[5], (D, D), D ** -0.5, 0.1875, ((1, 4),)),
        "self_key": noise(key_list[6], (D, D), D ** -0.5, 0.1875, ((1, 4),)),
        "self_value": noise(key_list[7], (D, D), D ** -0.5, 0.1875, ((1, 4),)),
        "self_out": noise(key_list[8], (D, D), (max(D // 256, 1)) ** -0.5, 3.0, ((0, 4),)),
        "self_out_bias": noise(key_list[9], (D,), 0.5, 2.5, (), jnp.float32),
        "norm2_gain": jnp.clip(1.0 + 0.18 * jax.random.normal(key_list[10], (D,), jnp.float32), 0.1, 1.9),
        "norm2_bias": noise(key_list[11], (D,), 0.5, 2.5, (), jnp.float32),
        "cross_query": noise(key_list[12], (D, D), D ** -0.5, 0.1875, ((1, 4),)),
        "cross_key": noise(key_list[13], (D, D), D ** -0.5, 0.1875, ((1, 4),)),
        "cross_value": noise(key_list[14], (D, D), D ** -0.5, 0.1875, ((1, 4),)),
        "cross_out": noise(key_list[15], (D, D), (max(D // 32, 1)) ** -0.5, 1.0, ((0, 4),)),
        "cross_out_bias": noise(key_list[16], (D,), 0.5, 2.5, (), jnp.float32),
        "norm3_gain": jnp.clip(1.0 + 0.18 * jax.random.normal(key_list[17], (D,), jnp.float32), 0.1, 1.9),
        "norm3_bias": noise(key_list[18], (D,), 0.5, 2.5, (), jnp.float32),
        "mlp_in": noise(key_list[19], (D, FF), D ** -0.5, 0.1875, ((1, 4),)),
        "mlp_in_bias": noise(key_list[20], (FF,), 1.0, 4.0, ((0, 4),), jnp.float32),
        "mlp_out": noise(key_list[21], (FF, D), (FF // 2) ** -0.5, 0.125, ((0, 4),)),
        "mlp_out_bias": noise(key_list[22], (D,), 0.5, 2.5, (), jnp.float32),
        "cotangent": noise(key_list[23], (TOKENS, D), 1.0, 6.0, ((0, 8),)),
    }


@jax.custom_vjp
def low(v):
    return lax.optimization_barrier(v.astype(jnp.bfloat16)).astype(jnp.float32)

@jax.custom_vjp
def low_back(v):
    return v

def low_keep(v):
    return (low(v), None)

def low_pass(kept, grad):
    return (grad,)

def back_keep(v):
    return (v, None)

def back_low(kept, grad):
    return (low(grad),)
low.defvjp(low_keep, low_pass)
low_back.defvjp(back_keep, back_low)
highest_precision = lax.Precision.HIGHEST
epsilon = 1e-05

def product(left_side, right_side):
    return jnp.dot(left_side, right_side, precision=highest_precision, preferred_element_type=jnp.float32)

def heads_of(values):
    return values.reshape(values.shape[0], HEADS, HEAD_DIM)

def layer_norm(values, norm_gain, norm_shift):
    average = lax.optimization_barrier(jnp.mean(values, axis=-1, keepdims=True))
    center = values - average
    variance = lax.optimization_barrier(jnp.mean(center * center, axis=-1, keepdims=True))
    return center * lax.rsqrt(variance + epsilon) * norm_gain + norm_shift

def attend(queries, key_rows, value_rows, allowed):
    scores = jnp.einsum('qhe,khe->hqk', queries, key_rows, precision=highest_precision) * HEAD_DIM ** (-0.5)
    scores = low_back(scores)
    scores = jnp.where(allowed[None], scores, -1e+30)
    shares = low(jax.nn.softmax(scores, axis=-1))
    mixed = jnp.einsum('hqk,khe->qhe', shares, value_rows, precision=highest_precision)
    return mixed.reshape(queries.shape[0], D)

def item_layer(item_tokens, item_text, item_length, weights):
    norm1_gain, norm1_bias, self_query, self_key, self_value, self_out, self_out_bias, norm2_gain, norm2_bias, cross_query, cross_key, cross_value, cross_out, cross_out_bias, norm3_gain, norm3_bias, mlp_in, mlp_in_bias, mlp_out, mlp_out_bias = weights
    positions = jnp.arange(SEQ)
    causal = positions[:, None] >= positions[None, :]
    normed = low(layer_norm(item_tokens, norm1_gain, norm1_bias))
    queries = heads_of(low(low_back(product(normed, self_query))))
    key_rows = heads_of(low(low_back(product(normed, self_key))))
    value_rows = heads_of(low(low_back(product(normed, self_value))))
    mixed = low(low_back(attend(queries, key_rows, value_rows, causal)))
    hidden = item_tokens + low_back(product(mixed, self_out) + self_out_bias)
    normed = low(layer_norm(hidden, norm2_gain, norm2_bias))
    queries = heads_of(low(low_back(product(normed, cross_query))))
    key_rows = heads_of(low(low_back(product(item_text, cross_key))))
    value_rows = heads_of(low(low_back(product(item_text, cross_value))))
    allowed = jnp.broadcast_to(jnp.arange(TXT)[None, :] < item_length, (SEQ, TXT))
    mixed = low(low_back(attend(queries, key_rows, value_rows, allowed)))
    hidden = hidden + low_back(product(mixed, cross_out) + cross_out_bias)
    normed = low(layer_norm(hidden, norm3_gain, norm3_bias))
    inner = low_back(product(normed, mlp_in) + mlp_in_bias)
    active = low(jax.nn.gelu(inner, approximate=False))
    return hidden + low_back(product(active, mlp_out) + mlp_out_bias)

def forward(tokens, texts, weights, lengths):

    def one_item(packed):
        return item_layer(packed[0], packed[1], packed[2], weights)
    outputs = lax.map(jax.checkpoint(one_item), (tokens.reshape(ITEMS, SEQ, D), texts, lengths))
    return outputs.reshape(ITEMS * SEQ, D)

def reference(inputs, text_states, text_lengths, norm1_gain, norm1_bias, self_query, self_key, self_value, self_out, self_out_bias, norm2_gain, norm2_bias, cross_query, cross_key, cross_value, cross_out, cross_out_bias, norm3_gain, norm3_bias, mlp_in, mlp_in_bias, mlp_out, mlp_out_bias, cotangent):
    params = tuple((member.astype(jnp.float32) for member in (norm1_gain, norm1_bias, self_query, self_key, self_value, self_out, self_out_bias, norm2_gain, norm2_bias, cross_query, cross_key, cross_value, cross_out, cross_out_bias, norm3_gain, norm3_bias, mlp_in, mlp_in_bias, mlp_out, mlp_out_bias)))

    def layer_only(tokens, texts, weights):
        return forward(tokens, texts, weights, text_lengths)
    result, pullback = jax.vjp(layer_only, inputs.astype(jnp.float32), text_states.astype(jnp.float32), params)
    input_grad, text_grad, weight_grads = pullback(cotangent.astype(jnp.float32))
    return (result.astype(jnp.bfloat16), input_grad.astype(jnp.bfloat16), text_grad, weight_grads[0], weight_grads[1], weight_grads[2], weight_grads[3], weight_grads[4], weight_grads[5], weight_grads[6], weight_grads[7], weight_grads[8], weight_grads[9], weight_grads[10], weight_grads[11], weight_grads[12], weight_grads[13], weight_grads[14], weight_grads[15], weight_grads[16], weight_grads[17], weight_grads[18], weight_grads[19])
```

```python
import functools

import jax
import jax.numpy as jnp
from jax import lax
from jax.experimental import pallas as pl
from jax.experimental.pallas import tpu as pltpu
from jax.sharding import PartitionSpec as P

HEAD_DIM = 64
TXT = 128
SEQ = 1024
BLOCK = 256
WIDTH = 256
SCALING = HEAD_DIM ** (-0.5)
HIDDEN = -1e30
epsilon = 1e-05
bf16 = jnp.bfloat16
f32 = jnp.float32


def contract(left_side, right_side, left_dim, right_dim):
    return lax.dot_general(
        left_side, right_side, (((left_dim,), (right_dim,)), ((), ())), preferred_element_type=f32
    )


def head_masks(heads):
    column_head = lax.broadcasted_iota(jnp.int32, (1, heads * HEAD_DIM), 1) // HEAD_DIM
    return [(column_head == head).astype(f32).astype(bf16) for head in range(heads)]


def self_forward_kernel(query_ref, key_ref, value_ref, mixed_ref, sums_ref, turned_ref):
    seq_rows, width = query_ref.shape
    heads = width // HEAD_DIM
    block = min(BLOCK, seq_rows)
    masks = head_masks(heads)
    turned_ref[...] = value_ref[...].T
    key_pos = lax.broadcasted_iota(jnp.int32, (block, block), 0)
    query_pos = lax.broadcasted_iota(jnp.int32, (block, block), 1)
    allowed = key_pos <= query_pos
    for start in range(0, seq_rows, block):
        seen = start + block
        queries = query_ref[start:seen, :] * SCALING
        mixed = []
        for head in range(heads):
            scores = contract(key_ref[:seen, :], queries * masks[head], 1, 1)
            corner = jnp.where(allowed, scores[start:, :], HIDDEN)
            if start:
                scores = jnp.concatenate([scores[:start, :], corner], 0)
            else:
                scores = corner
            highest = jnp.max(scores, axis=0, keepdims=True)
            weights = jnp.exp(scores - highest)
            row_total = jnp.sum(weights, axis=0, keepdims=True)
            shares = (weights * (1.0 / row_total)).astype(bf16)
            rows = slice(head * HEAD_DIM, (head + 1) * HEAD_DIM)
            mixed.append(contract(turned_ref[rows, :seen], shares, 1, 0))
            sums_ref[head : head + 1, start:seen] = highest + jnp.log(row_total)
        mixed_ref[start:seen, :] = jnp.concatenate(mixed, 0).T.astype(bf16)


def self_backward_kernel(
    query_ref, key_ref, value_ref, grad_ref, sums_ref, dq_ref, dk_ref, dv_ref, turned_ref, dk_sum, dv_sum
):
    seq_rows, width = query_ref.shape
    heads = width // HEAD_DIM
    block = min(BLOCK, seq_rows)
    masks = head_masks(heads)
    turned_ref[...] = key_ref[...].T
    key_pos = lax.broadcasted_iota(jnp.int32, (block, block), 0)
    query_pos = lax.broadcasted_iota(jnp.int32, (block, block), 1)
    allowed = key_pos <= query_pos
    for start in range(seq_rows - block, -1, -block):
        seen = start + block
        queries = query_ref[start:seen, :] * SCALING
        grads = grad_ref[start:seen, :]
        query_parts, share_list, slope_list, query_list, grad_list = [], [], [], [], []
        for head in range(heads):
            one_query = queries * masks[head]
            one_grad = grads * masks[head]
            scores = contract(key_ref[:seen, :], one_query, 1, 1)
            corner = jnp.where(allowed, scores[start:, :], HIDDEN)
            if start:
                scores = jnp.concatenate([scores[:start, :], corner], 0)
            else:
                scores = corner
            shares = jnp.exp(scores - sums_ref[head : head + 1, start:seen])
            share_grad = contract(value_ref[:seen, :], one_grad, 1, 1)
            along = jnp.sum(shares * share_grad, axis=0, keepdims=True)
            slopes = (shares * (share_grad - along)).astype(bf16)
            rows = slice(head * HEAD_DIM, (head + 1) * HEAD_DIM)
            query_parts.append(contract(turned_ref[rows, :seen], slopes, 1, 0) * SCALING)
            share_list.append(shares.astype(bf16))
            slope_list.append(slopes)
            query_list.append(one_query)
            grad_list.append(one_grad)
        dq_ref[start:seen, :] = jnp.concatenate(query_parts, 0).T.astype(bf16)
        key_part = contract(jnp.concatenate(slope_list, 1), jnp.concatenate(query_list, 0), 1, 0)
        value_part = contract(jnp.concatenate(share_list, 1), jnp.concatenate(grad_list, 0), 1, 0)
        if seen == seq_rows:
            dk_sum[...] = key_part
            dv_sum[...] = value_part
        else:
            dk_sum[:seen, :] += key_part
            dv_sum[:seen, :] += value_part
    dk_ref[...] = dk_sum[...].astype(bf16)
    dv_ref[...] = dv_sum[...].astype(bf16)


def stack_heads(rows, masks):
    return jnp.concatenate([rows * mask for mask in masks], 0)


def cross_scores(stacked_keys, queries, length, heads):
    scores = contract(stacked_keys, queries * SCALING, 1, 1)
    slots = scores.shape[0] // heads
    inside = lax.broadcasted_iota(jnp.int32, (slots, scores.shape[1]), 0) < length
    return [
        jnp.where(inside, scores[head * slots : (head + 1) * slots, :], HIDDEN)
        for head in range(heads)
    ]


def cross_forward_kernel(lengths_ref, query_ref, key_ref, value_ref, mixed_ref, sums_ref):
    seq_rows, width = query_ref.shape
    heads = width // HEAD_DIM
    block = min(2 * BLOCK, seq_rows)
    masks = head_masks(heads)
    length = lengths_ref[pl.program_id(0)]
    stacked_keys = stack_heads(key_ref[...], masks)
    turned_values = stack_heads(value_ref[...], masks).T
    for start in range(0, seq_rows, block):
        queries = query_ref[start : start + block, :]
        shares = []
        for head, scores in enumerate(cross_scores(stacked_keys, queries, length, heads)):
            highest = jnp.max(scores, axis=0, keepdims=True)
            weights = jnp.exp(scores - highest)
            row_total = jnp.sum(weights, axis=0, keepdims=True)
            shares.append((weights * (1.0 / row_total)).astype(bf16))
            sums_ref[head : head + 1, start : start + block] = highest + jnp.log(row_total)
        mixed = contract(turned_values, jnp.concatenate(shares, 0), 1, 0)
        mixed_ref[start : start + block, :] = mixed.T.astype(bf16)


def cross_backward_kernel(
    lengths_ref, query_ref, key_ref, value_ref, grad_ref, sums_ref, dq_ref, dk_ref, dv_ref
):
    seq_rows, width = query_ref.shape
    heads = width // HEAD_DIM
    slots = key_ref.shape[0]
    block = min(2 * BLOCK, seq_rows)
    masks = head_masks(heads)
    length = lengths_ref[pl.program_id(0)]
    stacked_keys = stack_heads(key_ref[...], masks)
    stacked_values = stack_heads(value_ref[...], masks)
    turned_keys = stacked_keys.T
    key_sum, value_sum = None, None
    for start in range(0, seq_rows, block):
        queries = query_ref[start : start + block, :]
        grads = grad_ref[start : start + block, :]
        share_grads = contract(stacked_values, grads, 1, 1)
        share_list, slope_list = [], []
        for head, scores in enumerate(cross_scores(stacked_keys, queries, length, heads)):
            shares = jnp.exp(scores - sums_ref[head : head + 1, start : start + block])
            share_grad = share_grads[head * slots : (head + 1) * slots, :]
            along = jnp.sum(shares * share_grad, axis=0, keepdims=True)
            slope_list.append((shares * (share_grad - along)).astype(bf16))
            share_list.append(shares.astype(bf16))
        slopes = jnp.concatenate(slope_list, 0)
        query_part = contract(turned_keys, slopes, 1, 0) * SCALING
        dq_ref[start : start + block, :] = query_part.T.astype(bf16)
        key_part = contract(slopes, queries * SCALING, 1, 0)
        value_part = contract(jnp.concatenate(share_list, 0), grads, 1, 0)
        key_sum = key_part if key_sum is None else key_sum + key_part
        value_sum = value_part if value_sum is None else value_sum + value_part
    key_total, value_total = 0.0, 0.0
    for head in range(heads):
        mask = masks[head].astype(f32)
        key_total += key_sum[head * slots : (head + 1) * slots, :] * mask
        value_total += value_sum[head * slots : (head + 1) * slots, :] * mask
    dk_ref[...] = key_total.astype(bf16)
    dv_ref[...] = value_total.astype(bf16)


def block_spec(rows, width, first):
    return pl.BlockSpec((None, rows, width), lambda item, at, *_: (item, 0, first + at))


def sums_spec(heads, rows):
    return pl.BlockSpec((None, None, heads, rows), lambda item, at, *_: (item, at, 0, 0))


def kernel_params():
    return pltpu.CompilerParams(vmem_limit_bytes=48 * 1024 * 1024)


def self_forward(queries, key_rows, value_rows):
    items, rows, total = queries.shape
    width = min(WIDTH, total)
    blocks = total // width
    heads = width // HEAD_DIM
    return pl.pallas_call(
        self_forward_kernel,
        grid=(items, blocks),
        in_specs=[block_spec(rows, width, 0)] * 3,
        out_specs=[block_spec(rows, width, 0), sums_spec(heads, rows)],
        out_shape=[
            jax.ShapeDtypeStruct((items, rows, total), bf16),
            jax.ShapeDtypeStruct((items, blocks, heads, rows), f32),
        ],
        scratch_shapes=[pltpu.VMEM((width, rows), bf16)],
        compiler_params=kernel_params(),
        name="self_forward",
    )(queries, key_rows, value_rows)


def self_backward(queries, key_rows, value_rows, grads, sums_kept):
    items, rows, total = queries.shape
    width = min(WIDTH, total)
    blocks = total // width
    heads = width // HEAD_DIM
    return pl.pallas_call(
        self_backward_kernel,
        grid=(items, blocks),
        in_specs=[block_spec(rows, width, 0)] * 4 + [sums_spec(heads, rows)],
        out_specs=[block_spec(rows, width, 0)] * 3,
        out_shape=[jax.ShapeDtypeStruct((items, rows, total), bf16)] * 3,
        scratch_shapes=[
            pltpu.VMEM((width, rows), bf16),
            pltpu.VMEM((rows, width), f32),
            pltpu.VMEM((rows, width), f32),
        ],
        compiler_params=kernel_params(),
        name="self_backward",
    )(queries, key_rows, value_rows, grads, sums_kept)


def cross_forward(queries, key_rows, value_rows, lengths):
    items, rows, total = queries.shape
    slots = key_rows.shape[1]
    width = min(WIDTH, total)
    blocks = total // width
    heads = width // HEAD_DIM
    return pl.pallas_call(
        cross_forward_kernel,
        grid_spec=pltpu.PrefetchScalarGridSpec(
            num_scalar_prefetch=1,
            grid=(items, blocks),
            in_specs=[
                block_spec(rows, width, 0),
                block_spec(slots, width, 0),
                block_spec(slots, width, 0),
            ],
            out_specs=[block_spec(rows, width, 0), sums_spec(heads, rows)],
        ),
        out_shape=[
            jax.ShapeDtypeStruct(queries.shape, bf16),
            jax.ShapeDtypeStruct((items, blocks, heads, rows), f32),
        ],
        compiler_params=kernel_params(),
        name="cross_forward",
    )(lengths, queries, key_rows, value_rows)


def cross_backward(queries, key_rows, value_rows, lengths, grads, sums_kept):
    items, rows, total = queries.shape
    slots = key_rows.shape[1]
    width = min(WIDTH, total)
    blocks = total // width
    heads = width // HEAD_DIM
    return pl.pallas_call(
        cross_backward_kernel,
        grid_spec=pltpu.PrefetchScalarGridSpec(
            num_scalar_prefetch=1,
            grid=(items, blocks),
            in_specs=[
                block_spec(rows, width, 0),
                block_spec(slots, width, 0),
                block_spec(slots, width, 0),
                block_spec(rows, width, 0),
                sums_spec(heads, rows),
            ],
            out_specs=[
                block_spec(rows, width, 0),
                block_spec(slots, width, 0),
                block_spec(slots, width, 0),
            ],
        ),
        out_shape=[
            jax.ShapeDtypeStruct(queries.shape, bf16),
            jax.ShapeDtypeStruct((items, slots, total), bf16),
            jax.ShapeDtypeStruct((items, slots, total), bf16),
        ],
        compiler_params=kernel_params(),
        name="cross_backward",
    )(lengths, queries, key_rows, value_rows, grads, sums_kept)


def layer_stats(hidden):
    average = jnp.mean(hidden, axis=-1, keepdims=True)
    center = hidden - average
    variance = jnp.mean(center * center, axis=-1, keepdims=True)
    inverse = lax.rsqrt(variance + epsilon)
    return (center * inverse, inverse)


def norm_back(upstream, scaled, inverse, gain_vector):
    tilted = upstream * gain_vector
    return inverse * (
        tilted
        - jnp.mean(tilted, axis=-1, keepdims=True)
        - scaled * jnp.mean(tilted * scaled, axis=-1, keepdims=True)
    )


ROWS = 256
UNITS = 512


def row_block(rows, width):
    return pl.BlockSpec((rows, width), lambda at: (at, 0))


def whole_block(array):
    origin = (0,) * array.ndim
    return pl.BlockSpec(array.shape, lambda at: origin, pipeline_mode=pl.Buffered(1))


def unit_block(rows, width):
    return pl.BlockSpec((rows, width), lambda at: (0, at))


def line(vector):
    return vector.reshape(1, -1)


def shape_of(rows, width, dtype):
    return jax.ShapeDtypeStruct((rows, width), dtype)


class Gathered:
    def __init__(self, group, at, part):
        self.array = group
        self.at = at
        self.part = part
        self.shape = (group.shape[0] * group.shape[1] * part, group.shape[3])

    def spec(self):
        dp, mp, _, width = self.array.shape
        place = self.at
        return pl.BlockSpec(
            (dp, mp, self.part, width), lambda at: (0, 0, place, 0), pipeline_mode=pl.Buffered(1)
        )

    def put_in_order(self, part_ref, held_ref):
        dp, mp = self.array.shape[:2]
        for at_mp in range(mp):
            for at_dp in range(dp):
                start = (at_mp * dp + at_dp) * self.part
                held_ref[start : start + self.part, :] = part_ref[at_dp, at_mp]


def by_rows(body, name, row_ins, weights, vectors, outs, sums=0):
    rows, width = row_ins[0].shape[0], row_ins[-1].shape[1]
    block = min(ROWS, rows)
    vectors = [line(each) for each in vectors]
    counts = [len(row_ins), len(weights), len(vectors), len(outs) + (sums > 0)]

    def kernel(*refs):
        groups = []
        for count in counts:
            groups.append(refs[:count])
            refs = refs[count:]
        held = list(refs)
        ready = []
        for weight, ref in zip(weights, groups[1]):
            if isinstance(weight, Gathered):
                target = held.pop(0)
                pl.when(pl.program_id(0) == 0)(functools.partial(weight.put_in_order, ref, target))
                ref = target
            ready.append(ref)
        body(groups[0], ready, groups[2], groups[3])

    weight_specs, weight_arrays, scratch = [], [], []
    for weight in weights:
        if isinstance(weight, Gathered):
            weight_specs.append(weight.spec())
            weight_arrays.append(weight.array)
            scratch.append(pltpu.VMEM(weight.shape, bf16))
        else:
            weight_specs.append(whole_block(weight))
            weight_arrays.append(weight)
    out_specs = [row_block(block, each.shape[1]) for each in outs]
    out_shapes = list(outs)
    if sums:
        out_specs.append(pl.BlockSpec((sums, width), lambda at: (0, 0)))
        out_shapes.append(shape_of(sums, width, f32))
    return pl.pallas_call(
        kernel,
        grid=(rows // block,),
        in_specs=[row_block(block, each.shape[1]) for each in row_ins]
        + weight_specs
        + [whole_block(each) for each in vectors],
        out_specs=out_specs,
        out_shape=out_shapes,
        scratch_shapes=scratch,
        compiler_params=kernel_params(),
        name=name,
    )(*row_ins, *weight_arrays, *vectors)


def norm_project(hidden, gain, shift, weights):
    def body(rows, weight_refs, vectors, outs):
        scaled, _ = layer_stats(rows[0][...].astype(f32))
        normed = (scaled * vectors[0][...] + vectors[1][...]).astype(bf16)
        outs[0][...] = normed
        for weight_ref, out_ref in zip(weight_refs, outs[1:]):
            out_ref[...] = contract(normed, weight_ref[...], 1, 1).astype(bf16)

    rows, width = hidden.shape
    outs = [shape_of(rows, width, bf16)] + [shape_of(rows, each.shape[0], bf16) for each in weights]
    return by_rows(body, "norm_project", [hidden], weights, [gain, shift], outs)


def add_branch(mixed, weight, before, add, gain, shift, following):
    def body(rows, weight_refs, vectors, outs):
        branch = contract(rows[0][...], weight_refs[0][...], 1, 0) + vectors[0][...]
        hidden = rows[1][...].astype(f32) + branch
        scaled, _ = layer_stats(hidden)
        normed = (scaled * vectors[1][...] + vectors[2][...]).astype(bf16)
        outs[0][...] = hidden
        outs[1][...] = normed
        for weight_ref, out_ref in zip(weight_refs[1:], outs[2:]):
            out_ref[...] = contract(normed, weight_ref[...], 1, 1).astype(bf16)

    rows, width = before.shape
    outs = [shape_of(rows, width, f32), shape_of(rows, width, bf16)]
    outs += [shape_of(rows, each.shape[0], bf16) for each in following]
    return by_rows(
        body, "add_branch", [mixed, before], [weight, *following], [add, gain, shift], outs
    )


def products(left, weights):
    def body(rows, weight_refs, vectors, outs):
        for weight_ref, out_ref in zip(weight_refs, outs):
            out_ref[...] = contract(rows[0][...], weight_ref[...], 1, 1).astype(bf16)

    outs = [shape_of(left.shape[0], each.shape[0], bf16) for each in weights]
    return by_rows(body, "products", [left], weights, [], outs)


def side_sum(sides, weights):
    total = contract(sides[0][...], weights[0][...], 1, 0)
    for side, weight in zip(sides[1:], weights[1:]):
        total = total + contract(side[...], weight[...], 1, 0)
    return total


def sum_products(sides, weights):
    def body(rows, weight_refs, vectors, outs):
        outs[0][...] = side_sum(rows, weight_refs).astype(bf16)

    outs = [shape_of(sides[0].shape[0], weights[0].shape[1], bf16)]
    return by_rows(body, "sum_products", sides, weights, [], outs)[0]


def layer_output(near, far, near_weight, far_weight, before, add):
    mp, chips, part, width = near_weight.shape

    def body(rows, weight_refs, vectors, outs):
        total = rows[2][...] + vectors[0][...]
        for side, weight in zip(rows[:2], weight_refs):
            for at in range(chips):
                columns = side[:, at * mp * part : (at + 1) * mp * part]
                total = total + contract(columns, weight[:, at].reshape(mp * part, width), 1, 0)
        outs[0][...] = total.astype(bf16)

    outs = [shape_of(*before.shape, bf16)]
    return by_rows(
        body, "layer_output", [near, far, before], [near_weight, far_weight], [add], outs
    )[0]


def norm_grad(sides, weights, hidden, above, gain, following):
    count = len(sides)

    def body(rows, weight_refs, vectors, outs):
        upstream = side_sum(rows[:count], weight_refs[:count])
        scaled, inverse = layer_stats(rows[count][...].astype(f32))
        above_rows = rows[count + 1][...].astype(f32)
        grad = above_rows + norm_back(upstream, scaled, inverse, vectors[0][...])
        low = grad.astype(bf16)
        outs[0][...] = low
        if following is not None:
            outs[1][...] = grad
            outs[2][...] = contract(low, weight_refs[count][...], 1, 1).astype(bf16)
        sums_ref = outs[-1]

        @pl.when(pl.program_id(0) == 0)
        def _():
            sums_ref[...] = jnp.zeros_like(sums_ref)

        for at, each in enumerate([upstream * scaled, upstream, low.astype(f32), above_rows]):
            sums_ref[at : at + 1, :] += jnp.sum(each, axis=0, keepdims=True)

    rows, width = hidden.shape
    outs = [shape_of(rows, width, bf16)]
    if following is not None:
        weights = [*weights, following]
        outs += [shape_of(rows, width, f32), shape_of(rows, following.shape[0], bf16)]
    return by_rows(body, "norm_grad", [*sides, hidden, above], weights, [gain], outs, sums=8)


def units_kernel(normed_ref, weight_ref, bias_ref, active_ref, slope_ref):
    rows = normed_ref.shape[0]
    block = min(ROWS, rows)
    for start in range(0, rows, block):
        at = slice(start, start + block)
        inner = contract(normed_ref[at, :], weight_ref[...], 1, 1) + bias_ref[...]
        below = 0.5 * (1.0 + lax.erf(inner * (0.5**0.5)))
        slope = below + inner * (jnp.exp(-0.5 * inner * inner) * 0.3989422804014327)
        active_ref[at, :] = (inner * below).astype(bf16)
        slope_ref[at, :] = slope.astype(bf16)


def hidden_units(normed, weight, bias):
    rows, width = normed.shape
    units = weight.shape[0]
    block = min(UNITS, units)
    return pl.pallas_call(
        units_kernel,
        grid=(units // block,),
        in_specs=[whole_block(normed), row_block(block, width), unit_block(1, block)],
        out_specs=[unit_block(rows, block)] * 2,
        out_shape=[shape_of(rows, units, bf16)] * 2,
        compiler_params=kernel_params(),
        name="hidden_units",
    )(normed, weight, line(bias))


def units_grad_kernel(
    active_ref, slope_ref, weight_ref, top_ref, normed_ref, inner_ref, out_ref, in_ref, sums_ref
):
    top = top_ref[...]
    out_ref[...] = contract(active_ref[...], top, 0, 0).astype(bf16)
    weight = weight_ref[...].reshape(-1, top.shape[1])
    inner = contract(top, weight, 1, 1) * slope_ref[...].astype(f32)
    inner = inner.astype(bf16)
    inner_ref[...] = inner
    sums_ref[...] = jnp.sum(inner.astype(f32), axis=0, keepdims=True)
    in_ref[...] = contract(inner, normed_ref[...], 0, 0).astype(bf16)


def units_grad(active, slope, weight, top, normed):
    rows, width = top.shape
    mp, chips, part = weight.shape[:3]
    units, block = mp * chips * part, mp * part
    return pl.pallas_call(
        units_grad_kernel,
        grid=(units // block,),
        in_specs=[unit_block(rows, block)] * 2
        + [
            pl.BlockSpec((mp, None, part, width), lambda at: (0, at, 0, 0)),
            whole_block(top),
            whole_block(normed),
        ],
        out_specs=[
            unit_block(rows, block),
            row_block(block, width),
            row_block(block, width),
            unit_block(1, block),
        ],
        out_shape=[
            shape_of(rows, units, bf16),
            shape_of(units, width, bf16),
            shape_of(units, width, bf16),
            shape_of(1, units, f32),
        ],
        compiler_params=kernel_params(),
        name="units_grad",
    )(active, slope, weight, top, normed)


def deal_kernel(mp, dp, own_ref, *refs):
    operands, outs = refs[: 2 * len(refs) // 3], refs[2 * len(refs) // 3 :]
    core, chip = own_ref[0] % 2, own_ref[0] // 2
    for at in range(len(operands) // 2):
        near_ref, far_ref = outs[at // 2 * 2], outs[at // 2 * 2 + 1]
        product = contract(operands[2 * at][...], operands[2 * at + 1][...], 0, 0).astype(bf16)
        part = product.shape[0] // (mp * dp)
        for at_mp in range(mp):
            for at_chip in range(dp // 2):
                start = (at_mp * dp + 2 * at_chip) * part
                even = product[start : start + part, :]
                odd = product[start + part : start + 2 * part, :]
                place = at_chip ^ chip
                near_ref[place, at_mp, at % 2] = jnp.where(core == 0, even, odd)
                far_ref[place, at_mp, at % 2] = jnp.where(core == 0, odd, even)


def deal_grads(*factors):
    mp, dp = lax.axis_size("mp"), lax.axis_size("dp")
    features, width = factors[0][0].shape[1], factors[0][1].shape[1]
    shape = (dp // 2, mp, 2, features // (mp * dp), width)
    operands = [each for pair in factors for each in pair]
    once = pl.Buffered(1)
    return pl.pallas_call(
        functools.partial(deal_kernel, mp, dp),
        grid_spec=pltpu.PrefetchScalarGridSpec(
            num_scalar_prefetch=1,
            grid=(1,),
            in_specs=[
                pl.BlockSpec(each.shape, lambda at, own: (0, 0), pipeline_mode=once)
                for each in operands
            ],
            out_specs=[
                pl.BlockSpec(shape, lambda at, own: (0, 0, 0, 0, 0), pipeline_mode=once)
                for _ in factors
            ],
        ),
        out_shape=[jax.ShapeDtypeStruct(shape, bf16) for _ in factors],
        compiler_params=kernel_params(),
        name="deal_grads",
    )(lax.axis_index("dp").reshape(1), *operands)


def column_part(shard):
    share = shard.shape[1] // lax.axis_size("dp")
    return lax.dynamic_slice_in_dim(shard, lax.axis_index("dp") * share, share, 1).T


def row_part(shard):
    share = shard.shape[0] // lax.axis_size("dp")
    return lax.dynamic_slice_in_dim(shard, lax.axis_index("dp") * share, share, 0)


def swap(value, axis, mask):
    count = lax.axis_size(axis)
    return lax.ppermute(value, axis, [(at, at ^ mask) for at in range(count)])


def chip_masks():
    return list(range(2, lax.axis_size("dp"), 2))


def tie(value, *others):
    anywhere = pl.BlockSpec(memory_space=pl.ANY)
    return pl.pallas_call(
        lambda *refs: None,
        in_specs=[anywhere] * (1 + len(others)),
        out_specs=anywhere,
        out_shape=jax.ShapeDtypeStruct(value.shape, value.dtype),
        input_output_aliases={0: 0},
        name="tie",
    )(value, *others)


def tie_all(values, *others):
    anywhere = pl.BlockSpec(memory_space=pl.ANY)
    return pl.pallas_call(
        lambda *refs: None,
        in_specs=[anywhere] * (len(values) + len(others)),
        out_specs=[anywhere] * len(values),
        out_shape=[jax.ShapeDtypeStruct(each.shape, each.dtype) for each in values],
        input_output_aliases={at: at for at in range(len(values))},
        name="tie_all",
    )(*values, *others)


def arrived(values, after):
    return tie_all(values, *after) if after else values


def gather_mp(value, axis=0, after=()):
    pieces = [swap(value, "mp", mask) for mask in range(1, lax.axis_size("mp"))]
    return jnp.stack([value, *arrived(pieces, after)], axis)


def low_sum(*terms):
    total = terms[0].astype(f32)
    for term in terms[1:]:
        total = total + term.astype(f32)
    return total.astype(bf16)


class PairSum:
    def __init__(self, terms, axis, unit, up):
        self.axis, self.unit = axis, unit
        count = terms[0].shape[0]
        bits = [1 << at for at in range(count.bit_length() - 1)]
        self.left = bits[::-1]
        self.order = bits if up else bits[::-1]
        self.terms = [each.reshape((2,) * len(bits) + each.shape[1:]) for each in terms]

    def step(self, after=()):
        bit, *self.order = self.order
        place = self.left.index(bit)
        self.left.remove(bit)
        sent = low_sum(*[lax.index_in_dim(each, 1, place, keepdims=False) for each in self.terms])
        [taken] = arrived([swap(sent, self.axis, self.unit * bit)], after)
        kept = [lax.index_in_dim(each, 0, place, keepdims=False) for each in self.terms]
        self.terms = kept + [taken]
        return taken

    def total(self, after=()):
        while self.order:
            self.step(after)
        return low_sum(*self.terms)


class PlaneSum(PairSum):
    def __init__(self, near, far, up):
        self.near, self.far, self.up = near, far, up

    def core(self, after=()):
        [taken] = arrived([swap(self.far, "dp", 1)], after)
        super().__init__([self.near, taken], "dp", 2, self.up)
        return taken

    def total(self, after=()):
        summed = super().total(after)
        return summed.reshape(summed.shape[0], -1, summed.shape[-1])


def over_mp(pieces):
    return PairSum([pieces], "mp", 1, True)


def spread(part, after=(), after_core=()):
    taken = [swap(part, "dp", mask) for mask in chip_masks()]
    near = jnp.stack([part, *arrived(taken, after)], 0)
    return jnp.concatenate([near, *arrived([swap(near, "dp", 1)], after_core)], 0)


def places_of_dp():
    apart = jnp.arange(lax.axis_size("dp"), dtype=jnp.int32) ^ lax.axis_index("dp")
    return (apart % 2) * (lax.axis_size("dp") // 2) + apart // 2


def settle_kernel(from_ref, *refs):
    refs[-1][...] = from_ref[...]


def settle(gathered, at, count, into=None):
    rows, width = gathered.shape
    block = rows // lax.axis_size("mp")
    before = [] if into is None else [into]
    return pl.pallas_call(
        settle_kernel,
        grid=(rows // block,),
        in_specs=[row_block(block, width)] + [pl.BlockSpec(memory_space=pl.ANY)] * len(before),
        out_specs=pl.BlockSpec((block, width), lambda step: (step * count + at, 0)),
        out_shape=shape_of(rows * count, width, gathered.dtype),
        input_output_aliases={1: 0} if before else {},
        compiler_params=kernel_params(),
        name="settle",
    )(gathered, *before)


def place_kernel(places_ref, part_ref, whole_ref):
    whole_ref[...] = part_ref[...].astype(f32)


def place(pieces, places):
    count, rows, width = pieces.shape
    return pl.pallas_call(
        place_kernel,
        grid_spec=pltpu.PrefetchScalarGridSpec(
            num_scalar_prefetch=1,
            grid=(count,),
            in_specs=[pl.BlockSpec((None, rows, width), lambda at, places: (places[at], 0, 0))],
            out_specs=pl.BlockSpec((rows, width), lambda at, places: (at, 0)),
        ),
        out_shape=shape_of(count * rows, width, f32),
        compiler_params=kernel_params(),
        name="place",
    )(places, pieces)


def finish_kernel(turned, places_ref, part_ref, whole_ref):
    count = part_ref.shape[0]
    rows = jnp.concatenate([part_ref[places_ref[at]] for at in range(count)], 0).astype(f32)
    whole_ref[...] = rows.T if turned else rows


def finish(value, places, first, rows, turned):
    count, total, width = value.shape
    value = value.reshape(count, total // rows, rows, width)
    at = first // rows
    shape = (width, count * rows) if turned else (count * rows, width)
    return pl.pallas_call(
        functools.partial(finish_kernel, turned),
        grid_spec=pltpu.PrefetchScalarGridSpec(
            num_scalar_prefetch=1,
            grid=(1,),
            in_specs=[pl.BlockSpec((count, None, rows, width), lambda i, places: (0, at, 0, 0))],
            out_specs=pl.BlockSpec(shape, lambda i, places: (0, 0)),
        ),
        out_shape=jax.ShapeDtypeStruct(shape, f32),
        compiler_params=kernel_params(),
        name="finish",
    )(places, value)


def on_device(
    inputs,
    text_states,
    text_lengths,
    norm1_gain,
    norm1_bias,
    self_query,
    self_key,
    self_value,
    self_out,
    self_out_bias,
    norm2_gain,
    norm2_bias,
    cross_query,
    cross_key,
    cross_value,
    cross_out,
    cross_out_bias,
    norm3_gain,
    norm3_bias,
    mlp_in,
    mlp_in_bias,
    mlp_out,
    mlp_out_bias,
    cotangent,
):
    mp, dp = lax.axis_size("mp"), lax.axis_size("dp")
    at_mp = lax.axis_index("mp")
    items_here = text_states.shape[0]
    width = inputs.shape[1]
    copies = max(1, mp // items_here)
    own_items = max(1, items_here // mp)
    first_item = (at_mp // copies) * own_items
    own_rows = own_items * SEQ

    def own(whole, count):
        return lax.dynamic_slice_in_dim(whole, first_item * count, own_items * count, 0)

    def counted(value):
        if copies == 1:
            return value
        return value * (at_mp % copies == 0).astype(value.dtype)

    def share_of(local):
        if copies == 1:
            return local
        part = local.shape[0] // copies
        return lax.dynamic_slice_in_dim(local, (at_mp % copies) * part, part, 0)

    def share_halves(local):
        local = share_of(local)
        half_rows = local.shape[0] // 2
        return [
            lax.all_gather(local[at * half_rows : (at + 1) * half_rows], "mp", axis=0, tiled=True)
            for at in range(2)
        ]

    def by_item(rows):
        return rows.reshape(own_items, -1, rows.shape[-1])

    part_of = self_query.shape[1] // dp
    hidden_part = mlp_in.shape[1] // dp
    at_dp = lax.axis_index("dp")
    near_indices = jnp.asarray([0] + chip_masks(), jnp.int32) ^ at_dp
    parts = jnp.concatenate([column_part(self_query), column_part(self_key), column_part(self_value)], 0)
    over_mp_self = gather_mp(parts)
    parts = jnp.concatenate(
        [
            tie(row_part(self_out), over_mp_self),
            column_part(cross_query),
            column_part(cross_key),
            column_part(cross_value),
            row_part(cross_out),
        ],
        0,
    )
    over_mp_cross = gather_mp(parts)
    self_group = lax.all_gather(over_mp_self, "dp", axis=0, tiled=False)
    self_weights = [Gathered(self_group, at, part_of) for at in range(3)]
    half = jnp.concatenate(
        [
            lax.dynamic_slice_in_dim(mlp_out, (at_dp ^ mask) * hidden_part, hidden_part, 0)[None]
            for mask in [0] + chip_masks()
        ],
        0,
    )

    tokens = own(inputs, SEQ)
    lengths = own(text_lengths, 1)
    texts = own(text_states, 1).reshape(own_items * TXT, width)
    grad_top = own(cotangent, SEQ)
    bias_whole = gather_mp(mlp_in_bias)
    gain = tie(norm1_gain, bias_whole)
    normed_self, *projected = norm_project(tokens, gain, norm1_bias, self_weights)
    cross_group = lax.all_gather(over_mp_cross, "dp", axis=0, tiled=False)
    self_out_whole, cross_query_whole, cross_key_whole, cross_value_whole, cross_out_whole = [
        Gathered(cross_group, at, part_of) for at in range(5)
    ]
    projected = [by_item(each) for each in projected]
    over_mp_in = gather_mp(tie(column_part(mlp_in), over_mp_cross), 0, [normed_self])
    half = tie(half, normed_self)
    self_mixed, self_sums = self_forward(*projected)
    mixed_rows = self_mixed.reshape(own_rows, width)
    over_mp_in = tie(over_mp_in, self_mixed)
    in_pieces = [swap(over_mp_in, "dp", mask) for mask in chip_masks()]
    hidden_one, normed_cross, cross_queries = add_branch(
        mixed_rows, self_out_whole, tokens, self_out_bias, norm2_gain, norm2_bias, [cross_query_whole]
    )
    cross_queries = by_item(cross_queries)
    cross_keys, cross_values = products(texts, [cross_key_whole, cross_value_whole])
    cross_keys, cross_values = by_item(cross_keys), by_item(cross_values)
    cross_mixed, cross_sums = cross_forward(cross_queries, cross_keys, cross_values, lengths)
    cross_rows = cross_mixed.reshape(own_rows, width)
    in_near = jnp.stack([over_mp_in, *tie_all(in_pieces, cross_mixed)], 0)
    in_far = swap(in_near, "dp", 1).reshape(-1, width)
    in_near = in_near.reshape(-1, width)
    hidden_two, normed_mlp = add_branch(
        cross_rows, cross_out_whole, hidden_one, cross_out_bias, norm3_gain, norm3_bias, []
    )
    bias_whole = bias_whole.reshape(mp, dp, hidden_part)
    bias_near = jnp.swapaxes(bias_whole[:, near_indices], 0, 1).reshape(-1)
    bias_far = jnp.swapaxes(bias_whole[:, near_indices ^ 1], 0, 1).reshape(-1)
    active_near, slope_near = hidden_units(normed_mlp, in_near, bias_near)
    out_near = gather_mp(half, 0, [active_near])
    out_far = swap(out_near, "dp", 1)
    active_far, slope_far = hidden_units(normed_mlp, in_far, bias_far)

    output = layer_output(active_near, active_far, out_near, out_far, hidden_two, mlp_out_bias)
    slope_far = tie(slope_far, output)
    output_halves = share_halves(output)
    inner_far, *far_parts, far_sums = units_grad(active_far, slope_far, out_far, grad_top, normed_mlp)
    inner_near, *near_parts, near_sums = units_grad(active_near, slope_near, out_near, grad_top, normed_mlp)

    def units_sum(which, up):
        halves = [
            counted(each[which]).reshape(dp // 2, mp, hidden_part, width)
            for each in (near_parts, far_parts)
        ]
        return PlaneSum(*halves, up)

    out_sum, in_sum = units_sum(0, True), units_sum(1, False)
    gain = tie(norm3_gain, out_sum.core([near_sums]), in_sum.core([near_sums]))
    branch_grad, hidden_two_grad, mixed_grad, sums_three = norm_grad(
        [inner_near, inner_far], [in_near, in_far], hidden_two, grad_top, gain, cross_out_whole
    )
    cross_sums = tie(cross_sums, out_sum.step([sums_three]), in_sum.step([sums_three]))
    query_grad, key_grad, value_grad = cross_backward(
        cross_queries, cross_keys, cross_values, lengths, by_item(mixed_grad), cross_sums
    )
    query_grad = query_grad.reshape(own_rows, width)
    key_grad = key_grad.reshape(own_items * TXT, width)
    value_grad = value_grad.reshape(own_items * TXT, width)

    def dealt_sums(*factors):
        near_a, far_a, near_b, far_b = [counted(each) for each in deal_grads(*factors)]
        return PlaneSum(near_a, far_a, True), PlaneSum(near_b, far_b, False)

    cross_a, cross_b = dealt_sums(
        (cross_rows, branch_grad), (query_grad, normed_cross), (key_grad, texts), (value_grad, texts)
    )
    text_grad = sum_products([key_grad, value_grad], [cross_key_whole, cross_value_whole])
    dealt = [cross_a.far]
    mlp_total = jnp.concatenate([out_sum.total(dealt), in_sum.total(dealt)], 1)
    gain = tie(norm2_gain, mlp_total, text_grad, output_halves[0])
    output = settle(output_halves[0], 0, 2)
    branch_grad, hidden_one_grad, mixed_grad, sums_two = norm_grad(
        [query_grad], [cross_query_whole], hidden_one, hidden_two_grad, gain, self_out_whole
    )
    text_sides = swap(share_of(text_grad)[None], "mp", mp // 2)
    text_sides = jnp.concatenate([share_of(text_grad)[None], *arrived([text_sides], [sums_two])], 0)
    self_sums = tie(self_sums, text_sides, cross_a.core([sums_two]), cross_b.core([sums_two]))
    side_grads = self_backward(*projected, by_item(mixed_grad), self_sums)
    side_grads = [each.reshape(own_rows, width) for each in side_grads]
    side = [side_grads[0]]
    mlp_sum = over_mp(mlp_total)
    bits = [mp // 2]
    while bits[-1] > 1:
        bits.append(bits[-1] // 2)
        text_sides = jnp.concatenate([text_sides, *arrived([swap(text_sides, "mp", bits[-1])], side)], 0)
    output = settle(output_halves[1], 1, 2, output)
    gain = tie(norm1_gain, output_halves[1], cross_a.step(side), cross_b.step(side), mlp_sum.step(side), text_sides)
    input_grad, sums_one = norm_grad(side_grads, self_weights, tokens, hidden_one_grad, gain, None)
    input_halves = share_halves(input_grad)
    input_grad = settle(input_halves[0], 0, 2)
    input_start = input_grad[:8, :128]
    input_grad = settle(input_halves[1], 1, 2, input_grad)
    mp_places = jnp.arange(mp, dtype=jnp.int32) ^ at_mp
    text_places = sum(((mp_places // bit) % 2) << at for at, bit in enumerate(bits))
    text_grad = place(text_sides, text_places)

    normed = [sums_one]
    cross_total = jnp.concatenate([cross_a.total(normed), cross_b.total(normed)], 1)
    mlp_part = mlp_sum.total(normed)
    value_side = tie(side_grads[2], sums_one, cross_total, mlp_part)
    self_a, self_b = dealt_sums(
        (side_grads[0], normed_self),
        (side_grads[1], normed_self),
        (value_side, normed_self),
        (mixed_rows, branch_grad),
    )
    dealt = [self_a.near]
    cross_part = over_mp(cross_total).total(dealt)
    mlp_parts = spread(mlp_part, dealt)
    self_a.core()
    self_b.core()
    self_total = jnp.concatenate([self_a.total(), self_b.total()], 1)
    cross_parts = spread(cross_part)
    late = spread(over_mp(self_total).total())
    places = places_of_dp()
    late_places = tie(places, input_start)
    mlp_out_grad = finish(mlp_parts, places, 0, hidden_part, False)
    mlp_in_grad = finish(mlp_parts, places, hidden_part, hidden_part, True)
    cross_out_grad, cross_query_grad, cross_key_grad, cross_value_grad = [
        finish(cross_parts, places, at * part_of, part_of, at > 0) for at in range(4)
    ]
    self_query_grad, self_key_grad, self_value_grad, self_out_grad = [
        finish(late, late_places, at * part_of, part_of, at < 3) for at in range(4)
    ]

    inner_sums = jnp.concatenate([near_sums, far_sums], 0).reshape(dp, mp, hidden_part)
    inner_sums = jnp.swapaxes(inner_sums[places][:, mp_places], 0, 1).reshape(-1, width)
    vectors = [sums_three[3], sums_three[0], sums_three[1], sums_three[2], sums_two[0], sums_two[1]]
    vectors += [sums_two[2], sums_one[0], sums_one[1]]
    sums = counted(jnp.concatenate([jnp.stack(vectors), inner_sums], 0))
    for axis, count in (("mp", mp), ("dp", dp)):
        reach = 1
        while reach < count:
            sums = sums + swap(sums, axis, reach)
            reach *= 2
    units_here = mlp_in_bias.shape[0]
    mlp_in_bias_grad = lax.dynamic_slice_in_dim(
        sums[len(vectors) :].reshape(-1), at_mp * units_here, units_here, 0
    )
    return (
        output,
        input_grad,
        text_grad.reshape(text_states.shape),
        sums[7],
        sums[8],
        self_query_grad,
        self_key_grad,
        self_value_grad,
        self_out_grad,
        sums[6],
        sums[4],
        sums[5],
        cross_query_grad,
        cross_key_grad,
        cross_value_grad,
        cross_out_grad,
        sums[3],
        sums[1],
        sums[2],
        mlp_in_grad,
        mlp_in_bias_grad,
        mlp_out_grad,
        sums[0],
    )


def solution(mesh):
    rows, column, row, everywhere = P("dp", None), P(None, "mp"), P("mp", None), P()
    return jax.shard_map(
        on_device,
        mesh=mesh,
        in_specs=(
            rows,
            P("dp", None, None),
            P("dp"),
            everywhere,
            everywhere,
            column,
            column,
            column,
            row,
            everywhere,
            everywhere,
            everywhere,
            column,
            column,
            column,
            row,
            everywhere,
            everywhere,
            everywhere,
            column,
            P("mp"),
            row,
            everywhere,
            rows,
        ),
        out_specs=(
            rows,
            rows,
            P("dp", None, None),
            everywhere,
            everywhere,
            column,
            column,
            column,
            row,
            everywhere,
            everywhere,
            everywhere,
            column,
            column,
            column,
            row,
            everywhere,
            everywhere,
            everywhere,
            column,
            P("mp"),
            row,
            everywhere,
        ),
        check_vma=False,
    )
```
